768 devices in a mesh: row: 192 (over z, y, core), col: 4 (over x).
Axes of the slice: x: 4, y: 8, z: 12, core: 2. Of those that a mesh axis runs over, the one named last changes fastest.
Arguments:
- slab: bfloat16 [2, 49152, 6144], P(None, 'row', 'col'), may hold values from 0.049804688 to 1
- slab_fill: int32 [2, 384, 48], P(None, 'row', 'col'), may hold values from 0 to 1, as said below
- panel: bfloat16 [2, 6144, 512], P(None, 'row', 'col'), may hold values from 0.049804688 to 1
- out_fill: int32 [384, 4], P('row', 'col'), may hold values from 0 to 1, as said below
Outputs:
- inflated: float32 [49152, 512], P('row', 'col')
The draws below stay inside these ranges and needn't reach their ends.
Inputs may be any that keep to these rules, and one draw needn't show every extreme that they name: `slab_fill`: in every section and block row, each aligned group of 12 tile columns (one index of col) holds 1 to 6 filled tiles, and some group of each section holds exactly 6. `out_fill`: every block column holds at least one kept tile.
All inputs are finite; a program needn't handle non-finite values.
Results may differ from the reference program's by a relative error of at most 0.0003.
Values may be sent and summed in bfloat16 or wider, within the bound.
No kernel may reach another device: no remote copies, remote signals or barrier semaphores. Data moves between devices by JAX's collectives and lax.ppermute only.
A program may use at most 64 MiB of HBM per device.

```python
import math
import jax
import jax.numpy as jnp
from jax import lax

TILE = 128
SECTIONS = 2
RB = 2
NRB = 384
NR = 49152
K_PANEL = 6144
KBLK = 48
NJB = 4
NJ = 512
N_ROW = 192
N_COL = 4


def draw_slab_fill(key, part):
    key = jax.random.fold_in(key, 11)
    key_count, key_score, key_pick = jax.random.split(key, 3)
    group_size = KBLK // N_COL
    slot_count = (group_size + 1) // 2
    counts = jax.random.randint(key_count, (SECTIONS, NRB, N_COL), 1, slot_count + 1)
    chosen = jax.random.randint(key_pick, (SECTIONS,), 0, NRB * N_COL)
    places = jnp.arange(NRB * N_COL, dtype=jnp.int32).reshape(NRB, N_COL)
    counts = jnp.where(places[None, :, :] == chosen[:, None, None], slot_count, counts)
    scores = jax.random.randint(key_score, (SECTIONS, NRB, N_COL, group_size), 0, 2 ** 20) * group_size
    scores = scores + jnp.arange(group_size, dtype=jnp.int32)
    ranking = jnp.argsort(jnp.argsort(scores, axis=-1), axis=-1)
    filled = (ranking < counts[..., None]).astype(jnp.int32)
    return filled.reshape(SECTIONS, NRB, KBLK)


def draw_out_fill(key, part):
    key = jax.random.fold_in(key, 23)
    key_bits, key_pick = jax.random.split(key, 2)
    random_bits = jax.random.randint(key_bits, (NRB, NJB), 0, 2)
    chosen = jax.random.randint(key_pick, (NJB,), 0, NRB)
    forced = jnp.arange(NRB, dtype=jnp.int32)[:, None] == chosen[None, :]
    return jnp.where(forced, 1, random_bits).astype(jnp.int32)


def block_levels(stream_key, extent, cuts, smallest, high):
    gain = 1.0
    for axis_at, parts in cuts:
        heights = jax.random.uniform(jax.random.fold_in(jax.random.fold_in(stream_key, 6), axis_at), (parts,), jnp.float32, smallest / len(cuts), high / len(cuts))
        gain = gain * jnp.repeat(jnp.exp(heights), extent[axis_at] // parts).reshape((-1,) + (1,) * (len(extent) - 1 - axis_at))
    return gain


def setup_inputs(seed: int = 0) -> dict:
    keys = jax.random.split(jax.random.key(seed), 5)
    return {
        "slab": jnp.clip(jnp.exp(math.log(1.0) - 2.9996462 * jax.random.uniform(keys[0], (SECTIONS, NR, K_PANEL), jnp.float32) ** block_levels(keys[0], (SECTIONS, NR, K_PANEL), ((1, 192), (2, 4)), -0.2, 0.2)), 0.049804688, 1.0).astype(jnp.bfloat16),
        "slab_fill": draw_slab_fill(jax.random.fold_in(keys[4], 71), 0),
        "panel": jnp.clip(jnp.exp(math.log(1.0) - 2.9996462 * jax.random.uniform(keys[2], (SECTIONS, K_PANEL, NJ), jnp.float32) ** block_levels(keys[2], (SECTIONS, K_PANEL, NJ), ((1, 192), (2, 4)), -0.2, 0.2)), 0.049804688, 1.0).astype(jnp.bfloat16),
        "out_fill": draw_out_fill(jax.random.fold_in(keys[4], 71), 0),
    }


def reference(slab, slab_fill, panel, out_fill):
    row_count = RB * TILE

    def one_group(group_index):
        slab_rows = lax.dynamic_slice_in_dim(slab, group_index * row_count, row_count, 1)
        fill_rows = lax.dynamic_slice_in_dim(slab_fill, group_index * RB, RB, 1)
        tile_mask = jnp.repeat(jnp.repeat(fill_rows, TILE, axis=1), TILE, axis=2).astype(jnp.bfloat16)
        masked = slab_rows * tile_mask
        product = jnp.zeros((row_count, NJ), jnp.float32)
        for step_index in range(SECTIONS):
            product = product + jnp.dot(masked[step_index], panel[step_index], preferred_element_type=jnp.float32)
        kept_rows = lax.dynamic_slice_in_dim(out_fill, group_index * RB, RB, 0)
        out_mask = jnp.repeat(jnp.repeat(kept_rows, TILE, axis=0), TILE, axis=1).astype(jnp.float32)
        return product * product * out_mask

    squares = lax.map(one_group, jnp.arange(N_ROW, dtype=jnp.int32))
    column_sums = jnp.sum(squares, axis=(0, 1))
    factor_col = jnp.float32(NR) / column_sums
    return (squares * factor_col).reshape(NR, NJ)
```

```python
import jax
import jax.numpy as jnp
from jax import lax
from jax.sharding import Mesh, PartitionSpec as P

TILE = 128
NZ, NY, NC, NX = 12, 8, 2, 4


def spread(piece, axis, size):
    copies = jnp.broadcast_to(piece[None], (size,) + piece.shape)
    return lax.all_to_all(copies, axis, 0, 0, tiled=True)


def shards(slab, slab_fill, panel, out_fill):
    sections, row_count, local_cols = slab.shape
    depth, width = panel.shape[1], panel.shape[2]
    tile_mask = jnp.repeat(jnp.repeat(slab_fill, TILE, axis=1), TILE, axis=2).astype(jnp.bfloat16)
    masked = slab * tile_mask
    moves = [
        (z * NX + x, ((z % 3) * 4 + x) * NX + z // 3) for z in range(NZ) for x in range(NX)
    ]
    piece = lax.ppermute(panel, ("z", "x"), moves)
    piece = spread(piece, "z", NZ)
    piece = spread(piece, "y", NY)
    piece = spread(piece, "core", NC)
    piece = piece.reshape(NC, NY, 3, NX, sections, depth, width)
    right = piece.transpose(4, 2, 1, 0, 5, 3, 6).reshape(sections, local_cols, NX * width)
    product = jnp.einsum("srk,skn->rn", masked, right, preferred_element_type=jnp.float32)
    product = product.reshape(row_count, NX, width).transpose(1, 0, 2)
    product = jnp.sum(lax.all_to_all(product, "x", 0, 0, tiled=True), axis=0)
    out_mask = jnp.repeat(jnp.repeat(out_fill, TILE, axis=0), TILE, axis=1).astype(jnp.float32)
    squares = product * product * out_mask
    sums = jnp.sum(squares.reshape(-1, 8, width), axis=0)
    sums = jnp.sum(spread(sums, ("y", "core"), NY * NC), axis=0)
    sums = jnp.sum(spread(sums, "z", NZ), axis=(0, 1))
    factor_col = jnp.float32(row_count * NZ * NY * NC) / sums
    return squares * factor_col


def solution(mesh):
    fine = Mesh(mesh.devices.reshape(NZ, NY, NC, NX), ("z", "y", "core", "x"))
    row = ("z", "y", "core")
    placed = (P(None, row, "x"), P(None, row, "x"), P(None, row, "x"), P(row, "x"))
    return jax.shard_map(
        shards, mesh=fine, in_specs=placed, out_specs=P(row, "x"), check_vma=False
    )
```

```python
import jax
import jax.numpy as jnp
from jax import lax
from jax.experimental import pallas as pl
from jax.experimental.pallas import tpu as pltpu
from jax.sharding import PartitionSpec as P

TILE = 128
NZ, NY, NC, NX = 12, 8, 2, 4


def row_of(z, y, core):
    return (z % NZ) * NY * NC + (y % NY) * NC + core


def spread(piece, axis, size, groups):
    copies = jnp.broadcast_to(piece[None], (size,) + piece.shape)
    return lax.all_to_all(copies, axis, 0, 0, tiled=True, axis_index_groups=groups)


def first_moves(turn):
    moves = []
    for z in range(NZ):
        for y in range(NY):
            for core in range(NC):
                for x in range(NX):
                    plane, third = z // 3, z % 3
                    target = row_of(x + 4 * ((third + turn) % 3), y, core)
                    moves.append((row_of(z, y, core) * NX + x, target * NX + plane))
    return moves


def step_of(position, shift):
    if shift == 2:
        return 2 if position % 2 == 0 else -2
    return shift


def shift_moves(shift):
    moves = []
    for z in range(NZ):
        for y in range(NY):
            moves.append((row_of(z, y, 0), row_of(z, y + step_of(y, shift), 0)))
            moves.append((row_of(z, y, 1), row_of(z + step_of(z, shift), y, 1)))
    return moves


SHIFTS = (0, 1, -1, 2)
MIXED_GROUPS = [
    [row_of(4 * a + j, b + 4 * h, 0) for j in range(4) for h in range(2)]
    for a in range(3)
    for b in range(4)
] + [[row_of(z, y, 1) for y in range(NY)] for z in range(NZ)]
PLANE_GROUPS = [[row_of(z, j // 2, j % 2) for j in range(NY * NC)] for z in range(NZ)]
Z_GROUPS = [[row_of(z, j // 2, j % 2) for z in range(NZ)] for j in range(NY * NC)]
SWAP = [(r, r ^ 1) for r in range(NZ * NY * NC)]


def places(row):
    z, y = row // (NY * NC), (row // NC) % NY
    shift = jnp.arange(4).reshape(4, 1, 1)
    slot = jnp.arange(8).reshape(1, 8, 1)
    turn = jnp.arange(3).reshape(1, 1, 3)

    def origin(position, size):
        two = jnp.where(position % 2 == 0, position - 2, position + 2)
        out = jnp.where(shift == 0, position, jnp.where(shift == 1, position - 1, position + 1))
        return (jnp.where(shift == 3, two, out) + size) % size

    y_from = origin(y, NY)
    z_from = origin(z, NZ)
    y0, c0 = y_from % 4 + 4 * (slot % 2), slot // 2
    third0 = (z // 4 - turn + 3) % 3
    y1, c1 = slot, z_from % 4
    third1 = (z_from // 4 - turn + 3) % 3
    k0 = (third0 * 16 + y0 * 2) * 32
    k1 = (third1 * 16 + y1 * 2 + 1) * 32
    full = (4, 8, 3)
    k = jnp.stack([jnp.broadcast_to(k0, full), jnp.broadcast_to(k1, full)])
    c = jnp.stack([jnp.broadcast_to(c0, full), jnp.broadcast_to(c1, full)])
    mine = row % NC
    flip = jnp.where(mine == 0, jnp.stack([k, c], -1), jnp.stack([k[::-1], c[::-1]], -1))
    return flip.reshape(-1).astype(jnp.int32)


def product_kernel(place_ref, fill_ref, slab_ref, *refs):
    pieces, out_ref, right_ref, left_ref = refs[:8], refs[8], refs[9], refs[10]
    sections = slab_ref.shape[0]
    for index, piece in enumerate(pieces):

        @pl.loop(0, 8)
        def _(slot, index=index, piece=piece):
            for turn in range(3):
                at = ((index * 8 + slot) * 3 + turn) * 2
                first = pl.multiple_of(place_ref[at], 32)
                column = pl.multiple_of(place_ref[at + 1] * TILE, TILE)
                for s in range(sections):
                    right_ref[s, pl.ds(first, 32), pl.ds(column, TILE)] = piece[slot, turn, s]

    rows, cols = slab_ref.shape[1] // TILE, slab_ref.shape[2] // TILE
    for s in range(sections):
        for r in range(rows):
            for k in range(cols):
                at = (s, slice(r * TILE, (r + 1) * TILE), slice(k * TILE, (k + 1) * TILE))
                keep = fill_ref[(s * rows + r) * cols + k].astype(jnp.float32).astype(jnp.bfloat16)
                left_ref[at] = slab_ref[at] * keep
    for r in range(rows):
        block = slice(r * TILE, (r + 1) * TILE)
        total = jnp.dot(left_ref[0, block], right_ref[0], preferred_element_type=jnp.float32)
        for s in range(1, sections):
            total += jnp.dot(left_ref[s, block], right_ref[s], preferred_element_type=jnp.float32)
        for c in range(NX):
            out_ref[c, block] = total[:, c * TILE : (c + 1) * TILE]


def multiply(place, fill, slab, pieces):
    sections, rows, cols = slab.shape
    smem = pl.BlockSpec(memory_space=pltpu.SMEM)
    vmem = pl.BlockSpec(memory_space=pltpu.VMEM)
    return pl.pallas_call(
        product_kernel,
        out_shape=jax.ShapeDtypeStruct((NX, rows, TILE), jnp.float32),
        in_specs=[smem, smem, vmem] + [vmem] * 8,
        out_specs=vmem,
        scratch_shapes=[
            pltpu.VMEM((sections, cols, NX * TILE), jnp.bfloat16),
            pltpu.VMEM((sections, rows, cols), jnp.bfloat16),
        ],
        compiler_params=pltpu.CompilerParams(vmem_limit_bytes=32 * 2**20),
        cost_estimate=pl.CostEstimate(
            flops=2 * sections * rows * cols * NX * TILE, bytes_accessed=5 * 2**20, transcendentals=0
        ),
    )(place, fill, slab, *pieces)


def shards(slab, slab_fill, panel, out_fill):
    sections, row_count, local_cols = slab.shape
    width = panel.shape[2]
    row = lax.axis_index("row")
    place = places(row)
    near = jnp.stack([lax.ppermute(panel, ("row", "col"), first_moves(t)) for t in range(3)])
    held = spread(near, "row", 8, MIXED_GROUPS).reshape(8, 3, sections, 32, width)
    mine = [held] + [lax.ppermute(held, "row", shift_moves(s)) for s in SHIFTS[1:]]
    theirs = [lax.ppermute(piece, "row", SWAP) for piece in mine]
    product = multiply(place, slab_fill.reshape(-1), slab, mine + theirs)
    product = jnp.sum(lax.all_to_all(product, "col", 0, 0, tiled=True), axis=0)
    out_mask = jnp.repeat(jnp.repeat(out_fill, TILE, axis=0), TILE, axis=1).astype(jnp.float32)
    squares = product * product * out_mask
    sums = jnp.sum(squares.reshape(-1, 8, width), axis=0)
    sums = jnp.sum(spread(sums, "row", NY * NC, PLANE_GROUPS), axis=0)
    sums = jnp.sum(spread(sums, "row", NZ, Z_GROUPS), axis=(0, 1))
    factor_col = jnp.float32(row_count * NZ * NY * NC) / sums
    return squares * factor_col


def solution(mesh):
    placed = (P(None, "row", "col"), P(None, "row", "col"), P(None, "row", "col"), P("row", "col"))
    return jax.shard_map(
        shards, mesh=mesh, in_specs=placed, out_specs=P("row", "col"), check_vma=False
    )
```

```python
import jax
import jax.numpy as jnp
from jax import lax
from jax.experimental import pallas as pl
from jax.experimental.pallas import tpu as pltpu
from jax.sharding import PartitionSpec as P

TILE = 128
NZ, NY, NC, NX = 12, 8, 2, 4
DEPTH = 32
SLOTS = 6
TAIL = 16


def row_of(z, y, core):
    return (z % NZ) * NY * NC + (y % NY) * NC + core


def spread(piece, axis, size, groups):
    copies = jnp.broadcast_to(piece[None], (size,) + piece.shape)
    return lax.all_to_all(copies, axis, 0, 0, tiled=True, axis_index_groups=groups)


def step_of(position, shift):
    if shift == 2:
        return 2 if position % 2 == 0 else -2
    return shift


def shift_moves(shift):
    moves = []
    for z in range(NZ):
        for y in range(NY):
            moves.append((row_of(z, y, 0), row_of(z, y + step_of(y, shift), 0)))
            moves.append((row_of(z, y, 1), row_of(z + step_of(z, shift), y, 1)))
    return moves


SHIFTS = (0, 1, -1, 2)
MIXED_GROUPS = [
    [row_of(z, b + 4 * h, 0) for z in range(NZ) for h in range(2)] for b in range(4)
] + [[row_of(j + 4 * i, y, 1) for i in range(3) for y in range(NY)] for j in range(4)]
GROUP = 24
PLANE_GROUPS = [[row_of(z, j // 2, j % 2) for j in range(NY * NC)] for z in range(NZ)]
Z_GROUPS = [[row_of(z, j // 2, j % 2) for z in range(NZ)] for j in range(NY * NC)]
SWAP = [(r, r ^ 1) for r in range(NZ * NY * NC)]


def pack_kernel(fill_ref, slab_ref, tail_ref, out_ref, tile_sems, tail_sem):
    sections, rows = slab_ref.shape[0], slab_ref.shape[1] // TILE
    cols = slab_ref.shape[2] // TILE

    def tile_copy(group, k, slot):
        s, r = group // rows, group % rows
        return pltpu.make_async_copy(
            slab_ref.at[s, pl.ds(r * TILE, TILE), pl.ds(k * TILE, TILE)],
            out_ref.at[pl.ds(group * TILE, TILE), pl.ds(pl.multiple_of(slot * TILE, TILE), TILE)],
            tile_sems.at[group, slot],
        )

    tail = pltpu.make_async_copy(
        tail_ref, out_ref.at[pl.ds(sections * rows * TILE, TAIL)], tail_sem
    )
    tail.start()
    for group in range(sections * rows):
        count = jnp.int32(0)
        for k in range(cols):
            count += fill_ref[group * cols + k]
        seen = jnp.int32(0)
        for k in range(cols):
            filled = fill_ref[group * cols + k]
            slot = jnp.where(filled == 1, seen, count + k - seen)
            seen += filled

            @pl.when(slot < SLOTS)
            def _(group=group, k=k, slot=slot):
                tile_copy(group, k, slot).start()

    for group in range(sections * rows):
        for slot in range(SLOTS):
            tile_copy(group, 0, slot).wait()
    tail.wait()


def pack(slab, slab_fill):
    sections, rows, cols = slab.shape
    groups = sections * rows // TILE
    fill = slab_fill.reshape(groups, cols // TILE)
    seen = jnp.cumsum(fill, axis=1) - fill
    count = jnp.sum(fill, axis=1, keepdims=True)
    k = jnp.arange(cols // TILE)[None, :]
    slot = jnp.where(fill == 1, seen, count + k - seen)
    hit = slot[:, None, :] == jnp.arange(SLOTS)[None, :, None]
    order = jnp.sum(jnp.where(hit, k[:, None, :], 0), axis=2)
    words = jnp.concatenate([order, count], axis=1).reshape(-1).astype(jnp.bfloat16)
    tail = jnp.pad(words[None, :], ((0, TAIL - 1), (0, SLOTS * TILE - words.shape[0])))
    anywhere = pl.BlockSpec(memory_space=pl.ANY)
    return pl.pallas_call(
        pack_kernel,
        out_shape=jax.ShapeDtypeStruct((groups * TILE + TAIL, SLOTS * TILE), jnp.bfloat16),
        in_specs=[pl.BlockSpec(memory_space=pltpu.SMEM), anywhere, anywhere],
        out_specs=anywhere,
        scratch_shapes=[pltpu.SemaphoreType.DMA((groups, SLOTS)), pltpu.SemaphoreType.DMA],
        cost_estimate=pl.CostEstimate(flops=0, bytes_accessed=2 * 2**20, transcendentals=0),
    )(fill.reshape(-1), slab, tail)


def product_kernel(place_ref, words_ref, keep_ref, *refs):
    lefts, pieces = refs[:NX], refs[NX : NX + 8]
    out_ref, sums_ref, right_ref, near_ref = refs[NX + 8 :]
    sections = right_ref.shape[0]
    row, col = place_ref[0], place_ref[1]
    z, y, core = row // (NY * NC), (row // NC) % NY, row % NC
    for index, piece in enumerate(pieces):
        step = index % 4
        if step == 3:
            y_from = jnp.where(y % 2 == 0, y - 2, y + 2)
            z_from = jnp.where(z % 2 == 0, z - 2, z + 2)
        else:
            y_from, z_from = y - SHIFTS[step], z - SHIFTS[step]
        along_y = (core == 0) == (index < 4)
        first = jnp.where(along_y, (y_from + NY) % 4 * 64, (z_from + NZ) % 4 * 512 + DEPTH)
        for slot in range(GROUP):
            offset = jnp.where(
                along_y, slot // 2 * 512 + slot % 2 * 256, slot // 8 * 2048 + slot % 8 * 64
            )
            at = pl.multiple_of(first + offset, DEPTH)
            for s in range(sections):
                right_ref[s, pl.ds(at, DEPTH)] = piece[slot, s]

    row_blocks = out_ref.shape[0] // TILE
    per_source = sections * row_blocks * (SLOTS + 1)
    colsum = jnp.zeros((8, TILE), jnp.float32)
    for r in range(row_blocks):
        total = jnp.zeros((TILE, TILE), jnp.float32)
        for source in range(NX):
            block_col = (col + (0, NX - 1, 1, 2)[source]) % NX
            for s in range(sections):
                group = s * row_blocks + r
                base = source * per_source + group * (SLOTS + 1)
                count = words_ref[base + SLOTS]
                parts = []
                for slot in range(SLOTS):
                    tile = block_col * 12 + words_ref[base + slot]
                    rows = pl.ds(pl.multiple_of(tile * TILE, TILE), TILE)
                    keep = (slot < count).astype(jnp.float32).astype(jnp.bfloat16)
                    near_ref[slot * TILE : (slot + 1) * TILE] = right_ref[s, rows] * keep
                left = lefts[source][group * TILE : (group + 1) * TILE, :]
                total += jnp.dot(left, near_ref[...], preferred_element_type=jnp.float32)
        squares = total * total * keep_ref[r].astype(jnp.float32)
        out_ref[r * TILE : (r + 1) * TILE] = squares
        colsum += jnp.sum(squares.reshape(TILE // 8, 8, TILE), axis=0)
    sums_ref[...] = jnp.broadcast_to(colsum[None], sums_ref.shape)


def multiply(place, words, keep, lefts, pieces, sections, rows):
    smem = pl.BlockSpec(memory_space=pltpu.SMEM)
    vmem = pl.BlockSpec(memory_space=pltpu.VMEM)
    depth = NZ * NY * NC * DEPTH
    return pl.pallas_call(
        product_kernel,
        out_shape=(
            jax.ShapeDtypeStruct((rows, TILE), jnp.float32),
            jax.ShapeDtypeStruct((NY * NC, 8, TILE), jnp.float32),
        ),
        in_specs=[smem, smem, smem] + [vmem] * (NX + 8),
        out_specs=(vmem, vmem),
        scratch_shapes=[
            pltpu.VMEM((sections, depth, TILE), jnp.bfloat16),
            pltpu.VMEM((SLOTS * TILE, TILE), jnp.bfloat16),
        ],
        compiler_params=pltpu.CompilerParams(vmem_limit_bytes=32 * 2**20),
        cost_estimate=pl.CostEstimate(
            flops=sections * rows * depth * TILE, bytes_accessed=7 * 2**20, transcendentals=0
        ),
    )(place, words, keep, *lefts, *pieces)


def shards(slab, slab_fill, panel, out_fill):
    sections, row_count, local_cols = slab.shape
    place = jnp.stack([lax.axis_index("row"), lax.axis_index("col")]).astype(jnp.int32)
    held = spread(panel, "row", GROUP, MIXED_GROUPS)
    packed = pack(slab, slab_fill)
    lefts = [packed] + [
        lax.ppermute(packed, "col", [(x, (x + s) % NX) for x in range(NX)]) for s in SHIFTS[1:]
    ]
    mine = [held] + [lax.ppermute(held, "row", shift_moves(s)) for s in SHIFTS[1:]]
    theirs = [lax.ppermute(piece, "row", SWAP) for piece in mine]
    tail = sections * row_count
    count = sections * row_count // TILE * (SLOTS + 1)
    words = jnp.concatenate([left[tail, :count] for left in lefts]).astype(jnp.int32)
    squares, sums = multiply(
        place, words, out_fill.reshape(-1), lefts, mine + theirs, sections, row_count
    )
    sums = lax.all_to_all(sums, "row", 0, 0, tiled=True, axis_index_groups=PLANE_GROUPS)
    sums = jnp.sum(sums, axis=0)
    sums = jnp.sum(spread(sums, "row", NZ, Z_GROUPS), axis=(0, 1))
    factor_col = jnp.float32(row_count * NZ * NY * NC) / sums
    return squares * factor_col


def solution(mesh):
    placed = (P(None, "row", "col"), P(None, "row", "col"), P(None, "row", "col"), P("row", "col"))
    return jax.shard_map(
        shards, mesh=mesh, in_specs=placed, out_specs=P("row", "col"), check_vma=False
    )
```

```python
import jax
import jax.numpy as jnp
from jax import lax
from jax.experimental import pallas as pl
from jax.experimental.pallas import tpu as pltpu
from jax.sharding import PartitionSpec as P

TILE = 128
NZ, NY, NC, NX = 12, 8, 2, 4
DEPTH = 32
SLOTS = 6
TAIL = 16


def row_of(z, y, core):
    return (z % NZ) * NY * NC + (y % NY) * NC + core


def spread(piece, axis, size, groups):
    copies = jnp.broadcast_to(piece[None], (size,) + piece.shape)
    return lax.all_to_all(copies, axis, 0, 0, tiled=True, axis_index_groups=groups)


def step_of(position, shift):
    if shift == 2:
        return 2 if position % 2 == 0 else -2
    return shift


def shift_moves(shift):
    moves = []
    for z in range(NZ):
        for y in range(NY):
            moves.append((row_of(z, y, 0), row_of(z, y + step_of(y, shift), 0)))
            moves.append((row_of(z, y, 1), row_of(z + step_of(z, shift), y, 1)))
    return moves


SHIFTS = (0, 1, -1, 2)
MIXED_GROUPS = [
    [row_of(z, b + 4 * h, 0) for z in range(NZ) for h in range(2)] for b in range(4)
] + [[row_of(j + 4 * i, y, 1) for i in range(3) for y in range(NY)] for j in range(4)]
GROUP = 24
PLANE_GROUPS = [[row_of(z, j // 2, j % 2) for j in range(NY * NC)] for z in range(NZ)]
Z_GROUPS = [[row_of(z, j // 2, j % 2) for z in range(NZ)] for j in range(NY * NC)]
SWAP = [(r, r ^ 1) for r in range(NZ * NY * NC)]


def pack_kernel(fill_ref, slab_ref, out_ref):
    sections, rows = slab_ref.shape[0], slab_ref.shape[1] // TILE
    cols = slab_ref.shape[2] // TILE
    lane = lax.broadcasted_iota(jnp.int32, (TAIL, TILE), 1)
    words = jnp.zeros((TAIL, TILE), jnp.float32)
    for group in range(sections * rows):
        s, r = group // rows, group % rows
        count = jnp.int32(0)
        for k in range(cols):
            count += fill_ref[s, r, k]
        seen = jnp.int32(0)
        for k in range(cols):
            filled = fill_ref[s, r, k]
            slot = jnp.where(filled == 1, seen, count + k - seen)
            seen += filled

            @pl.when(slot < SLOTS)
            def _(group=group, s=s, r=r, k=k, slot=slot):
                column = pl.multiple_of(slot * TILE, TILE)
                out_ref[pl.ds(group * TILE, TILE), pl.ds(column, TILE)] = slab_ref[
                    s, r * TILE : (r + 1) * TILE, k * TILE : (k + 1) * TILE
                ]

            place = jnp.where(slot < SLOTS, group * (SLOTS + 1) + slot, -1)
            words = jnp.where(lane == place, jnp.float32(k), words)
        words = jnp.where(lane == group * (SLOTS + 1) + SLOTS, count.astype(jnp.float32), words)
    tail = slice(sections * rows * TILE, sections * rows * TILE + TAIL)
    out_ref[tail, :] = jnp.zeros((TAIL, SLOTS * TILE), jnp.bfloat16)
    out_ref[tail, :TILE] = words.astype(jnp.bfloat16)


def pack(slab, slab_fill):
    sections, rows, cols = slab.shape
    height = sections * rows + TAIL
    vmem = pl.BlockSpec(memory_space=pltpu.VMEM)
    return pl.pallas_call(
        pack_kernel,
        out_shape=jax.ShapeDtypeStruct((height, SLOTS * TILE), jnp.bfloat16),
        in_specs=[pl.BlockSpec(memory_space=pltpu.SMEM), vmem],
        out_specs=vmem,
        compiler_params=pltpu.CompilerParams(vmem_limit_bytes=16 * 2**20),
        cost_estimate=pl.CostEstimate(flops=0, bytes_accessed=2 * 2**20, transcendentals=0),
    )(slab_fill, slab)


def product_kernel(place_ref, words_ref, keep_ref, *refs):
    lefts_ref, pieces = refs[0], refs[1:9]
    out_ref, sums_ref, right_ref, near_ref, left_ref, left_sem = refs[9:]
    fetch = pltpu.make_async_copy(lefts_ref, left_ref, left_sem)
    fetch.start()
    sections = right_ref.shape[0]
    row = place_ref[0]
    z, y, core = row // (NY * NC), (row // NC) % NY, row % NC
    for index, piece in enumerate(pieces):
        step = index % 4
        if step == 3:
            y_from = jnp.where(y % 2 == 0, y - 2, y + 2)
            z_from = jnp.where(z % 2 == 0, z - 2, z + 2)
        else:
            y_from, z_from = y - SHIFTS[step], z - SHIFTS[step]
        along_y = (core == 0) == (index < 4)
        first = jnp.where(along_y, (y_from + NY) % 4 * 64, (z_from + NZ) % 4 * 512 + DEPTH)
        for slot in range(GROUP):
            offset = jnp.where(
                along_y, slot // 2 * 512 + slot % 2 * 256, slot // 8 * 2048 + slot % 8 * 64
            )
            at = pl.multiple_of(first + offset, DEPTH)
            for s in range(sections):
                right_ref[s, pl.ds(at, DEPTH)] = piece[slot, s]

    fetch.wait()
    row_blocks = out_ref.shape[0] // TILE
    per_source = sections * row_blocks * (SLOTS + 1)
    colsum = jnp.zeros((8, TILE), jnp.float32)
    for r in range(row_blocks):
        total = jnp.zeros((TILE, TILE), jnp.float32)
        for source in range(NX):
            for s in range(sections):
                group = s * row_blocks + r
                base = source * per_source + group * (SLOTS + 1)
                count = words_ref[base + SLOTS]
                for slot in range(SLOTS):
                    tile = source * 12 + words_ref[base + slot]
                    rows = pl.ds(pl.multiple_of(tile * TILE, TILE), TILE)
                    keep = (slot < count).astype(jnp.float32).astype(jnp.bfloat16)
                    near_ref[slot * TILE : (slot + 1) * TILE] = right_ref[s, rows] * keep
                left = left_ref[source, group * TILE : (group + 1) * TILE, :]
                total += jnp.dot(left, near_ref[...], preferred_element_type=jnp.float32)
        squares = total * total * keep_ref[r].astype(jnp.float32)
        out_ref[r * TILE : (r + 1) * TILE] = squares
        colsum += jnp.sum(squares.reshape(TILE // 8, 8, TILE), axis=0)
    sums_ref[...] = jnp.broadcast_to(colsum[None], sums_ref.shape)


def multiply(place, words, keep, lefts, pieces, sections, rows):
    smem = pl.BlockSpec(memory_space=pltpu.SMEM)
    vmem = pl.BlockSpec(memory_space=pltpu.VMEM)
    depth = NZ * NY * NC * DEPTH
    return pl.pallas_call(
        product_kernel,
        out_shape=(
            jax.ShapeDtypeStruct((rows, TILE), jnp.float32),
            jax.ShapeDtypeStruct((NY * NC, 8, TILE), jnp.float32),
        ),
        in_specs=[smem, smem, smem] + [pl.BlockSpec(memory_space=pl.ANY)] + [vmem] * 8,
        out_specs=(vmem, vmem),
        scratch_shapes=[
            pltpu.VMEM((sections, depth, TILE), jnp.bfloat16),
            pltpu.VMEM((SLOTS * TILE, TILE), jnp.bfloat16),
            pltpu.VMEM(lefts.shape, jnp.bfloat16),
            pltpu.SemaphoreType.DMA,
        ],
        compiler_params=pltpu.CompilerParams(vmem_limit_bytes=32 * 2**20),
        cost_estimate=pl.CostEstimate(
            flops=sections * rows * depth * TILE, bytes_accessed=7 * 2**20, transcendentals=0
        ),
    )(place, words, keep, lefts, *pieces)


def shards(slab, slab_fill, panel, out_fill):
    sections, row_count, local_cols = slab.shape
    place = lax.axis_index("row").astype(jnp.int32).reshape(1)
    held = spread(panel, "row", GROUP, MIXED_GROUPS)
    lefts = lax.all_gather(pack(slab, slab_fill), "col", axis=0)
    mine = [held] + [lax.ppermute(held, "row", shift_moves(s)) for s in SHIFTS[1:]]
    theirs = [lax.ppermute(piece, "row", SWAP) for piece in mine]
    tail = sections * row_count
    count = sections * row_count // TILE * (SLOTS + 1)
    words = lefts[:, tail, :count].reshape(-1).astype(jnp.int32)
    squares, sums = multiply(
        place, words, out_fill.reshape(-1), lefts, mine + theirs, sections, row_count
    )
    sums = lax.all_to_all(sums, "row", 0, 0, tiled=True, axis_index_groups=PLANE_GROUPS)
    sums = jnp.sum(sums, axis=0)
    sums = jnp.sum(spread(sums, "row", NZ, Z_GROUPS), axis=(0, 1))
    factor_col = jnp.float32(row_count * NZ * NY * NC) / sums
    return squares * factor_col


def solution(mesh):
    placed = (P(None, "row", "col"), P(None, "row", "col"), P(None, "row", "col"), P("row", "col"))
    return jax.shard_map(
        shards, mesh=mesh, in_specs=placed, out_specs=P("row", "col"), check_vma=False
    )
```

```python
import jax
import jax.numpy as jnp
from jax import lax
from jax.experimental import pallas as pl
from jax.experimental.pallas import tpu as pltpu
from jax.sharding import PartitionSpec as P

TILE = 128
NZ, NY, NC, NX = 12, 8, 2, 4
DEPTH = 32
SLOTS = 6
TAIL = 16
HALF = 2


def row_of(z, y, core):
    return (z % NZ) * NY * NC + (y % NY) * NC + core


def spread(piece, axis, size, groups):
    copies = jnp.broadcast_to(piece[None], (size,) + piece.shape)
    return lax.all_to_all(copies, axis, 0, 0, tiled=True, axis_index_groups=groups)


def step_of(position, shift):
    if shift == 2:
        return 2 if position % 2 == 0 else -2
    return shift


def shift_moves(shift):
    moves = []
    for z in range(NZ):
        for y in range(NY):
            moves.append((row_of(z, y, 0), row_of(z, y + step_of(y, shift), 0)))
            moves.append((row_of(z, y, 1), row_of(z + step_of(z, shift), y, 1)))
    return moves


SHIFTS = (0, 1, -1, 2)
MIXED_GROUPS = [
    [row_of(z, b + 4 * h, 0) for z in range(NZ) for h in range(2)] for b in range(4)
] + [[row_of(j + 4 * i, y, 1) for i in range(3) for y in range(NY)] for j in range(4)]
GROUP = 24
PLANE_GROUPS = [[row_of(z, j // 2, j % 2) for j in range(NY * NC)] for z in range(NZ)]
Z_GROUPS = [[row_of(z, j // 2, j % 2) for z in range(NZ)] for j in range(NY * NC)]
UP = [(x, (x + 1) % NX) for x in range(NX)]
DOWN = [((x + 1) % NX, x) for x in range(NX)]
CORE_GROUPS = [[r, r + 1] for r in range(0, NZ * NY * NC, NC)]


def pack_kernel(fill_ref, slab_ref, out_ref):
    sections, rows = slab_ref.shape[0], slab_ref.shape[1] // TILE
    cols = slab_ref.shape[2] // TILE
    lane = lax.broadcasted_iota(jnp.int32, (TAIL, TILE), 1)
    words = jnp.zeros((TAIL, TILE), jnp.float32)
    for group in range(sections * rows):
        s, r = group // rows, group % rows
        count = jnp.int32(0)
        for k in range(cols):
            count += fill_ref[s, r, k]
        seen = jnp.int32(0)
        for k in range(cols):
            filled = fill_ref[s, r, k]
            slot = jnp.where(filled == 1, seen, count + k - seen)
            seen += filled

            @pl.when(slot < SLOTS)
            def _(group=group, s=s, r=r, k=k, slot=slot):
                column = pl.multiple_of(slot * TILE, TILE)
                out_ref[pl.ds(group * TILE, TILE), pl.ds(column, TILE)] = slab_ref[
                    s, r * TILE : (r + 1) * TILE, k * TILE : (k + 1) * TILE
                ]

            place = jnp.where(slot < SLOTS, group * (SLOTS + 1) + slot, -1)
            words = jnp.where(lane == place, jnp.float32(k), words)
        words = jnp.where(lane == group * (SLOTS + 1) + SLOTS, count.astype(jnp.float32), words)
    tail = slice(sections * rows * TILE, sections * rows * TILE + TAIL)
    out_ref[tail, :] = jnp.zeros((TAIL, SLOTS * TILE), jnp.bfloat16)
    out_ref[tail, :TILE] = words.astype(jnp.bfloat16)


def pack(slab, slab_fill):
    sections, rows, cols = slab.shape
    height = sections * rows + TAIL
    vmem = pl.BlockSpec(memory_space=pltpu.VMEM)
    return pl.pallas_call(
        pack_kernel,
        out_shape=jax.ShapeDtypeStruct((height, SLOTS * TILE), jnp.bfloat16),
        in_specs=[pl.BlockSpec(memory_space=pltpu.SMEM), vmem],
        out_specs=vmem,
        compiler_params=pltpu.CompilerParams(vmem_limit_bytes=16 * 2**20),
        cost_estimate=pl.CostEstimate(flops=0, bytes_accessed=2 * 2**20, transcendentals=0),
    )(slab_fill, slab)


def product_kernel(place_ref, words_ref, keep_ref, *refs):
    lefts, pieces = refs[:NX], refs[NX : NX + 4]
    out_ref, sums_ref, right_ref, near_ref = refs[NX + 4 :]
    sections = right_ref.shape[0]
    row, col = place_ref[0], place_ref[1]
    z, y = row // (NY * NC), (row // NC) % NY
    for step, piece in enumerate(pieces):
        if step == 3:
            y_from = jnp.where(y % 2 == 0, y - 2, y + 2)
            z_from = jnp.where(z % 2 == 0, z - 2, z + 2)
        else:
            y_from, z_from = y - SHIFTS[step], z - SHIFTS[step]
        first_y, first_z = (y_from + NY) % 4 * 64, (z_from + NZ) % 4 * 512
        for slot in range(GROUP):
            at_y = first_y + (slot // 2 * 512 + slot % 2 * 256)
            at_z = first_z + (slot // 8 * 2048 + slot % 8 * 64 + DEPTH)
            for core, at in enumerate((at_y, at_z)):
                rows = pl.ds(pl.multiple_of(at, DEPTH), DEPTH)
                for s in range(sections):
                    right_ref[s, rows] = piece[core, slot, s]

    row_blocks = out_ref.shape[0] // TILE
    per_source = sections * row_blocks * (SLOTS + 1)
    colsum = jnp.zeros((8, TILE), jnp.float32)
    for r in range(row_blocks):
        total = jnp.zeros((TILE, TILE), jnp.float32)
        for source in range(NX):
            block_col = (col + (0, NX - 1, 1, 2)[source]) % NX
            for s in range(sections):
                group = s * row_blocks + r
                base = source * per_source + group * (SLOTS + 1)
                count = words_ref[base + SLOTS]
                for slot in range(SLOTS):
                    tile = block_col * 12 + words_ref[base + slot]
                    rows = pl.ds(pl.multiple_of(tile * TILE, TILE), TILE)
                    keep = (slot < count).astype(jnp.float32).astype(jnp.bfloat16)
                    near_ref[slot * TILE : (slot + 1) * TILE] = right_ref[s, rows] * keep
                left = lefts[source][group * TILE : (group + 1) * TILE, :]
                total += jnp.dot(left, near_ref[...], preferred_element_type=jnp.float32)
        squares = total * total * keep_ref[r].astype(jnp.float32)
        out_ref[r * TILE : (r + 1) * TILE] = squares
        colsum += jnp.sum(squares.reshape(TILE // 8, 8, TILE), axis=0)
    sums_ref[...] = jnp.broadcast_to(colsum[None], sums_ref.shape)


def multiply(place, words, keep, lefts, pieces, sections, rows):
    smem = pl.BlockSpec(memory_space=pltpu.SMEM)
    vmem = pl.BlockSpec(memory_space=pltpu.VMEM)
    depth = NZ * NY * NC * DEPTH
    return pl.pallas_call(
        product_kernel,
        out_shape=(
            jax.ShapeDtypeStruct((rows, TILE), jnp.float32),
            jax.ShapeDtypeStruct((NY * NC, 8, TILE), jnp.float32),
        ),
        in_specs=[smem, smem, smem] + [vmem] * (NX + 4),
        out_specs=(vmem, vmem),
        scratch_shapes=[
            pltpu.VMEM((sections, depth, TILE), jnp.bfloat16),
            pltpu.VMEM((SLOTS * TILE, TILE), jnp.bfloat16),
        ],
        compiler_params=pltpu.CompilerParams(vmem_limit_bytes=32 * 2**20),
        cost_estimate=pl.CostEstimate(
            flops=sections * rows * depth * TILE, bytes_accessed=7 * 2**20, transcendentals=0
        ),
    )(place, words, keep, *lefts, *pieces)


def shards(slab, slab_fill, panel, out_fill):
    sections, row_count, local_cols = slab.shape
    place = jnp.stack([lax.axis_index("row"), lax.axis_index("col")]).astype(jnp.int32)
    held = spread(panel, "row", GROUP, MIXED_GROUPS)
    packed = pack(slab, slab_fill)
    lefts = [packed] + [
        lax.ppermute(packed, "col", [(x, (x + step) % NX) for x in range(NX)])
        for step in (1, NX - 1, 2)
    ]
    mine = [held] + [lax.ppermute(held, "row", shift_moves(s)) for s in SHIFTS[1:]]
    pieces = [lax.all_gather(piece, "row", axis_index_groups=CORE_GROUPS) for piece in mine]
    tail = sections * row_count
    count = sections * row_count // TILE * (SLOTS + 1)
    words = jnp.concatenate([left[tail, :count] for left in lefts]).astype(jnp.int32)
    squares, sums = multiply(
        place, words, out_fill.reshape(-1), lefts, pieces, sections, row_count
    )
    sums = lax.all_to_all(sums, "row", 0, 0, tiled=True, axis_index_groups=PLANE_GROUPS)
    sums = jnp.sum(sums, axis=0)
    sums = jnp.sum(spread(sums, "row", NZ, Z_GROUPS), axis=(0, 1))
    factor_col = jnp.float32(row_count * NZ * NY * NC) / sums
    return squares * factor_col


def solution(mesh):
    placed = (P(None, "row", "col"), P(None, "row", "col"), P(None, "row", "col"), P("row", "col"))
    return jax.shard_map(
        shards, mesh=mesh, in_specs=placed, out_specs=P("row", "col"), check_vma=False
    )
```

```python
import jax
import jax.numpy as jnp
from jax import lax
from jax.experimental import pallas as pl
from jax.experimental.pallas import tpu as pltpu
from jax.sharding import PartitionSpec as P

TILE = 128
NZ, NY, NC, NX = 12, 8, 2, 4
DEPTH = 32
SLOTS = 6
TAIL = 16
HALF = 2


def row_of(z, y, core):
    return (z % NZ) * NY * NC + (y % NY) * NC + core


def spread(piece, axis, size, groups):
    copies = jnp.broadcast_to(piece[None], (size,) + piece.shape)
    return lax.all_to_all(copies, axis, 0, 0, tiled=True, axis_index_groups=groups)


def step_of(position, shift):
    if shift == 2:
        return 2 if position % 2 == 0 else -2
    return shift


def shift_moves(shift):
    moves = []
    for z in range(NZ):
        for y in range(NY):
            moves.append((row_of(z, y, 0), row_of(z, y + step_of(y, shift), 0)))
            moves.append((row_of(z, y, 1), row_of(z + step_of(z, shift), y, 1)))
    return moves


SHIFTS = (0, 1, -1, 2)
MIXED_GROUPS = [
    [row_of(z, b + 4 * h, 0) for z in range(NZ) for h in range(2)] for b in range(4)
] + [[row_of(j + 4 * i, y, 1) for i in range(3) for y in range(NY)] for j in range(4)]
GROUP = 24
PLANE_GROUPS = [[row_of(z, j // 2, j % 2) for j in range(NY * NC)] for z in range(NZ)]
Z_GROUPS = [[row_of(z, j // 2, j % 2) for z in range(NZ)] for j in range(NY * NC)]
UP = [(x, (x + 1) % NX) for x in range(NX)]
DOWN = [((x + 1) % NX, x) for x in range(NX)]
CORE_GROUPS = [[r, r + 1] for r in range(0, NZ * NY * NC, NC)]


def pack_kernel(fill_ref, slab_ref, out_ref):
    sections, rows = slab_ref.shape[0], slab_ref.shape[1] // TILE
    cols = slab_ref.shape[2] // TILE
    lane = lax.broadcasted_iota(jnp.int32, (TAIL, TILE), 1)
    words = jnp.zeros((TAIL, TILE), jnp.float32)
    for group in range(sections * rows):
        s, r = group // rows, group % rows
        count = jnp.int32(0)
        for k in range(cols):
            count += fill_ref[s, r, k]
        seen = jnp.int32(0)
        for k in range(cols):
            filled = fill_ref[s, r, k]
            slot = jnp.where(filled == 1, seen, count + k - seen)
            seen += filled

            @pl.when(slot < SLOTS)
            def _(group=group, s=s, r=r, k=k, slot=slot):
                column = pl.multiple_of(slot * TILE, TILE)
                out_ref[pl.ds(group * TILE, TILE), pl.ds(column, TILE)] = slab_ref[
                    s, r * TILE : (r + 1) * TILE, k * TILE : (k + 1) * TILE
                ]

            place = jnp.where(slot < SLOTS, group * (SLOTS + 1) + slot, -1)
            words = jnp.where(lane == place, jnp.float32(k), words)
        words = jnp.where(lane == group * (SLOTS + 1) + SLOTS, count.astype(jnp.float32), words)
    tail = slice(sections * rows * TILE, sections * rows * TILE + TAIL)
    out_ref[tail, :] = jnp.zeros((TAIL, SLOTS * TILE), jnp.bfloat16)
    out_ref[tail, :TILE] = words.astype(jnp.bfloat16)


def pack(slab, slab_fill):
    sections, rows, cols = slab.shape
    height = sections * rows + TAIL
    vmem = pl.BlockSpec(memory_space=pltpu.VMEM)
    return pl.pallas_call(
        pack_kernel,
        out_shape=jax.ShapeDtypeStruct((height, SLOTS * TILE), jnp.bfloat16),
        in_specs=[pl.BlockSpec(memory_space=pltpu.SMEM), vmem],
        out_specs=vmem,
        compiler_params=pltpu.CompilerParams(vmem_limit_bytes=16 * 2**20),
        cost_estimate=pl.CostEstimate(flops=0, bytes_accessed=2 * 2**20, transcendentals=0),
    )(slab_fill, slab)


def product_kernel(place_ref, words_ref, keep_ref, *refs):
    lefts, pieces = refs[:NX], refs[NX : NX + 4]
    out_ref, sums_ref, right_ref, near_ref = refs[NX + 4 :]
    sections = right_ref.shape[0]
    row, col = place_ref[0], place_ref[1]
    z, y = row // (NY * NC), (row // NC) % NY
    for step, piece in enumerate(pieces):
        if step == 3:
            y_from = jnp.where(y % 2 == 0, y - 2, y + 2)
            z_from = jnp.where(z % 2 == 0, z - 2, z + 2)
        else:
            y_from, z_from = y - SHIFTS[step], z - SHIFTS[step]
        first_y, first_z = (y_from + NY) % 4 * 64, (z_from + NZ) % 4 * 512
        for slot in range(GROUP):
            at_y = first_y + (slot // 2 * 512 + slot % 2 * 256)
            at_z = first_z + (slot // 8 * 2048 + slot % 8 * 64 + DEPTH)
            for core, at in enumerate((at_y, at_z)):
                rows = pl.ds(pl.multiple_of(at, DEPTH), DEPTH)
                for s in range(sections):
                    right_ref[s, rows] = piece[core, slot, s]

    row_blocks = out_ref.shape[0] // TILE
    per_source = sections * row_blocks * (SLOTS + 1)
    colsum = jnp.zeros((8, TILE), jnp.float32)
    for r in range(row_blocks):
        total = jnp.zeros((TILE, TILE), jnp.float32)
        for source in range(NX):
            block_col = (col + (0, NX - 1, 1, 2)[source]) % NX
            for s in range(sections):
                group = s * row_blocks + r
                base = source * per_source + group * (SLOTS + 1)
                count = words_ref[base + SLOTS]
                for slot in range(SLOTS):
                    tile = block_col * 12 + words_ref[base + slot]
                    rows = pl.ds(pl.multiple_of(tile * TILE, TILE), TILE)
                    keep = (slot < count).astype(jnp.float32).astype(jnp.bfloat16)
                    near_ref[slot * TILE : (slot + 1) * TILE] = right_ref[s, rows] * keep
                left = lefts[source][group * TILE : (group + 1) * TILE, :]
                total += jnp.dot(left, near_ref[...], preferred_element_type=jnp.float32)
        squares = total * total * keep_ref[r].astype(jnp.float32)
        out_ref[r * TILE : (r + 1) * TILE] = squares
        colsum += jnp.sum(squares.reshape(TILE // 8, 8, TILE), axis=0)
    sums_ref[...] = jnp.broadcast_to(colsum[None], sums_ref.shape)


def multiply(place, words, keep, lefts, pieces, sections, rows):
    smem = pl.BlockSpec(memory_space=pltpu.SMEM)
    vmem = pl.BlockSpec(memory_space=pltpu.VMEM)
    depth = NZ * NY * NC * DEPTH
    return pl.pallas_call(
        product_kernel,
        out_shape=(
            jax.ShapeDtypeStruct((rows, TILE), jnp.float32),
            jax.ShapeDtypeStruct((NY * NC, 8, TILE), jnp.float32),
        ),
        in_specs=[smem, smem, smem] + [vmem] * (NX + 4),
        out_specs=(vmem, vmem),
        scratch_shapes=[
            pltpu.VMEM((sections, depth, TILE), jnp.bfloat16),
            pltpu.VMEM((SLOTS * TILE, TILE), jnp.bfloat16),
        ],
        compiler_params=pltpu.CompilerParams(vmem_limit_bytes=32 * 2**20),
        cost_estimate=pl.CostEstimate(
            flops=sections * rows * depth * TILE, bytes_accessed=7 * 2**20, transcendentals=0
        ),
    )(place, words, keep, *lefts, *pieces)


def shards(slab, slab_fill, panel, out_fill):
    sections, row_count, local_cols = slab.shape
    place = jnp.stack([lax.axis_index("row"), lax.axis_index("col")]).astype(jnp.int32)
    held = spread(panel, "row", GROUP, MIXED_GROUPS)
    packed = pack(slab, slab_fill)
    below = lax.ppermute(packed, "col", UP)
    above = lax.ppermute(packed, "col", DOWN)
    across = lax.ppermute(below, "col", UP)
    mine = [held] + [lax.ppermute(held, "row", shift_moves(s)) for s in SHIFTS[1:]]
    moved, (above, across) = lax.optimization_barrier((mine[1:], (above, across)))
    mine = [held] + moved
    lefts = [packed, below, above, across]
    pieces = [lax.all_gather(piece, "row", axis_index_groups=CORE_GROUPS) for piece in mine]
    tail = sections * row_count
    count = sections * row_count // TILE * (SLOTS + 1)
    words = jnp.concatenate([left[tail, :count] for left in lefts]).astype(jnp.int32)
    squares, sums = multiply(
        place, words, out_fill.reshape(-1), lefts, pieces, sections, row_count
    )
    sums = lax.all_to_all(sums, "row", 0, 0, tiled=True, axis_index_groups=PLANE_GROUPS)
    sums = jnp.sum(sums, axis=0)
    sums = jnp.sum(spread(sums, "row", NZ, Z_GROUPS), axis=(0, 1))
    factor_col = jnp.float32(row_count * NZ * NY * NC) / sums
    return squares * factor_col


def solution(mesh):
    placed = (P(None, "row", "col"), P(None, "row", "col"), P(None, "row", "col"), P("row", "col"))
    return jax.shard_map(
        shards, mesh=mesh, in_specs=placed, out_specs=P("row", "col"), check_vma=False
    )
```

```python
import jax
import jax.numpy as jnp
from jax import lax
from jax.experimental import pallas as pl
from jax.experimental.pallas import tpu as pltpu
from jax.sharding import PartitionSpec as P

TILE = 128
NZ, NY, NC, NX = 12, 8, 2, 4
DEPTH = 32
SLOTS = 6
TAIL = 16
HALF = 2


def row_of(z, y, core):
    return (z % NZ) * NY * NC + (y % NY) * NC + core


def spread(piece, axis, size, groups):
    copies = jnp.broadcast_to(piece[None], (size,) + piece.shape)
    return lax.all_to_all(copies, axis, 0, 0, tiled=True, axis_index_groups=groups)


def step_of(position, shift):
    if shift == 2:
        return 2 if position % 2 == 0 else -2
    return shift


def shift_moves(shift):
    moves = []
    for z in range(NZ):
        for y in range(NY):
            moves.append((row_of(z, y, 0), row_of(z, y + step_of(y, shift), 0)))
            moves.append((row_of(z, y, 1), row_of(z + step_of(z, shift), y, 1)))
    return moves


SHIFTS = (0, 2, 1, -1)
MIXED_GROUPS = [
    [row_of(z, b + 4 * h, 0) for z in range(NZ) for h in range(2)] for b in range(4)
] + [[row_of(j + 4 * i, y, 1) for i in range(3) for y in range(NY)] for j in range(4)]
GROUP = 24
PLANE_GROUPS = [[row_of(z, j // 2, j % 2) for j in range(NY * NC)] for z in range(NZ)]
Z_GROUPS = [[row_of(z, j // 2, j % 2) for z in range(NZ)] for j in range(NY * NC)]
UP = [(x, (x + 1) % NX) for x in range(NX)]
DOWN = [((x + 1) % NX, x) for x in range(NX)]
CORE_GROUPS = [[r, r + 1] for r in range(0, NZ * NY * NC, NC)]


def pack_kernel(fill_ref, slab_ref, out_ref):
    sections, rows = slab_ref.shape[0], slab_ref.shape[1] // TILE
    cols = slab_ref.shape[2] // TILE
    lane = lax.broadcasted_iota(jnp.int32, (TAIL, TILE), 1)
    words = jnp.zeros((TAIL, TILE), jnp.float32)
    for group in range(sections * rows):
        s, r = group // rows, group % rows
        count = jnp.int32(0)
        for k in range(cols):
            count += fill_ref[s, r, k]
        seen = jnp.int32(0)
        for k in range(cols):
            filled = fill_ref[s, r, k]
            slot = jnp.where(filled == 1, seen, count + k - seen)
            seen += filled

            @pl.when(slot < SLOTS)
            def _(group=group, s=s, r=r, k=k, slot=slot):
                column = pl.multiple_of(slot * TILE, TILE)
                out_ref[pl.ds(group * TILE, TILE), pl.ds(column, TILE)] = slab_ref[
                    s, r * TILE : (r + 1) * TILE, k * TILE : (k + 1) * TILE
                ]

            place = jnp.where(slot < SLOTS, group * (SLOTS + 1) + slot, -1)
            words = jnp.where(lane == place, jnp.float32(k), words)
        words = jnp.where(lane == group * (SLOTS + 1) + SLOTS, count.astype(jnp.float32), words)
    tail = slice(sections * rows * TILE, sections * rows * TILE + TAIL)
    out_ref[tail, :] = jnp.zeros((TAIL, SLOTS * TILE), jnp.bfloat16)
    out_ref[tail, :TILE] = words.astype(jnp.bfloat16)


def pack(slab, slab_fill):
    sections, rows, cols = slab.shape
    height = sections * rows + TAIL
    vmem = pl.BlockSpec(memory_space=pltpu.VMEM)
    return pl.pallas_call(
        pack_kernel,
        out_shape=jax.ShapeDtypeStruct((height, SLOTS * TILE), jnp.bfloat16),
        in_specs=[pl.BlockSpec(memory_space=pltpu.SMEM), vmem],
        out_specs=vmem,
        compiler_params=pltpu.CompilerParams(vmem_limit_bytes=16 * 2**20),
        cost_estimate=pl.CostEstimate(flops=0, bytes_accessed=2 * 2**20, transcendentals=0),
    )(slab_fill, slab)


def product_kernel(place_ref, words_ref, keep_ref, *refs):
    lefts, pieces = refs[:NX], refs[NX : NX + 4]
    out_ref, sums_ref, right_ref, near_ref = refs[NX + 4 :]
    sections = right_ref.shape[0]
    row, col = place_ref[0], place_ref[1]
    z, y = row // (NY * NC), (row // NC) % NY
    for step, piece in enumerate(pieces):
        if SHIFTS[step] == 2:
            y_from = jnp.where(y % 2 == 0, y - 2, y + 2)
            z_from = jnp.where(z % 2 == 0, z - 2, z + 2)
        else:
            y_from, z_from = y - SHIFTS[step], z - SHIFTS[step]
        first_y, first_z = (y_from + NY) % 4 * 64, (z_from + NZ) % 4 * 512
        for slot in range(GROUP):
            at_y = first_y + (slot // 2 * 512 + slot % 2 * 256)
            at_z = first_z + (slot // 8 * 2048 + slot % 8 * 64 + DEPTH)
            for core, at in enumerate((at_y, at_z)):
                rows = pl.ds(pl.multiple_of(at, DEPTH), DEPTH)
                for s in range(sections):
                    right_ref[s, rows] = piece[core, slot, s]

    row_blocks = out_ref.shape[0] // TILE
    per_source = sections * row_blocks * (SLOTS + 1)
    colsum = jnp.zeros((8, TILE), jnp.float32)
    for r in range(row_blocks):
        total = jnp.zeros((TILE, TILE), jnp.float32)
        for source in range(NX):
            block_col = (col + (0, NX - 1, 1, 2)[source]) % NX
            for s in range(sections):
                group = s * row_blocks + r
                base = source * per_source + group * (SLOTS + 1)
                count = words_ref[base + SLOTS]
                for slot in range(SLOTS):
                    tile = block_col * 12 + words_ref[base + slot]
                    rows = pl.ds(pl.multiple_of(tile * TILE, TILE), TILE)
                    keep = (slot < count).astype(jnp.float32).astype(jnp.bfloat16)
                    near_ref[slot * TILE : (slot + 1) * TILE] = right_ref[s, rows] * keep
                left = lefts[source][group * TILE : (group + 1) * TILE, :]
                total += jnp.dot(left, near_ref[...], preferred_element_type=jnp.float32)
        squares = total * total * keep_ref[r].astype(jnp.float32)
        out_ref[r * TILE : (r + 1) * TILE] = squares
        colsum += jnp.sum(squares.reshape(TILE // 8, 8, TILE), axis=0)
    sums_ref[...] = jnp.broadcast_to(colsum[None], sums_ref.shape)


def multiply(place, words, keep, lefts, pieces, sections, rows):
    smem = pl.BlockSpec(memory_space=pltpu.SMEM)
    vmem = pl.BlockSpec(memory_space=pltpu.VMEM)
    depth = NZ * NY * NC * DEPTH
    return pl.pallas_call(
        product_kernel,
        out_shape=(
            jax.ShapeDtypeStruct((rows, TILE), jnp.float32),
            jax.ShapeDtypeStruct((NY * NC, 8, TILE), jnp.float32),
        ),
        in_specs=[smem, smem, smem] + [vmem] * (NX + 4),
        out_specs=(vmem, vmem),
        scratch_shapes=[
            pltpu.VMEM((sections, depth, TILE), jnp.bfloat16),
            pltpu.VMEM((SLOTS * TILE, TILE), jnp.bfloat16),
        ],
        compiler_params=pltpu.CompilerParams(vmem_limit_bytes=32 * 2**20),
        cost_estimate=pl.CostEstimate(
            flops=sections * rows * depth * TILE, bytes_accessed=7 * 2**20, transcendentals=0
        ),
    )(place, words, keep, *lefts, *pieces)


def shards(slab, slab_fill, panel, out_fill):
    sections, row_count, local_cols = slab.shape
    place = jnp.stack([lax.axis_index("row"), lax.axis_index("col")]).astype(jnp.int32)
    held = spread(panel, "row", GROUP, MIXED_GROUPS)
    packed = pack(slab, slab_fill)
    below = lax.ppermute(packed, "col", UP)
    above = lax.ppermute(packed, "col", DOWN)
    across = lax.ppermute(below, "col", UP)
    mine = [held] + [lax.ppermute(held, "row", shift_moves(s)) for s in SHIFTS[1:]]
    moved, (above, across) = lax.optimization_barrier((mine[1:], (above, across)))
    mine = [held] + moved
    lefts = [packed, below, above, across]
    pieces = [lax.all_gather(piece, "row", axis_index_groups=CORE_GROUPS) for piece in mine]
    tail = sections * row_count
    count = sections * row_count // TILE * (SLOTS + 1)
    words = jnp.concatenate([left[tail, :count] for left in lefts]).astype(jnp.int32)
    squares, sums = multiply(
        place, words, out_fill.reshape(-1), lefts, pieces, sections, row_count
    )
    sums = lax.all_to_all(sums, "row", 0, 0, tiled=True, axis_index_groups=PLANE_GROUPS)
    sums = jnp.sum(sums, axis=0)
    sums = jnp.sum(spread(sums, "row", NZ, Z_GROUPS), axis=(0, 1))
    factor_col = jnp.float32(row_count * NZ * NY * NC) / sums
    return squares * factor_col


def solution(mesh):
    placed = (P(None, "row", "col"), P(None, "row", "col"), P(None, "row", "col"), P("row", "col"))
    return jax.shard_map(
        shards, mesh=mesh, in_specs=placed, out_specs=P("row", "col"), check_vma=False
    )
```

```python
import jax
import jax.numpy as jnp
from jax import lax
from jax.experimental import pallas as pl
from jax.experimental.pallas import tpu as pltpu
from jax.sharding import PartitionSpec as P

TILE = 128
NZ, NY, NC, NX = 12, 8, 2, 4
DEPTH = 32
SLOTS = 6
TAIL = 16
HALF = 2


def row_of(z, y, core):
    return (z % NZ) * NY * NC + (y % NY) * NC + core


def spread(piece, axis, size, groups):
    copies = jnp.broadcast_to(piece[None], (size,) + piece.shape)
    return lax.all_to_all(copies, axis, 0, 0, tiled=True, axis_index_groups=groups)


def step_of(position, shift):
    if shift == 2:
        return 2 if position % 2 == 0 else -2
    return shift


def shift_moves(shift):
    moves = []
    for z in range(NZ):
        for y in range(NY):
            moves.append((row_of(z, y, 0), row_of(z, y + step_of(y, shift), 0)))
            moves.append((row_of(z, y, 1), row_of(z + step_of(z, shift), y, 1)))
    return moves


SHIFTS = (0, 2, 1, -1)
MIXED_GROUPS = [
    [row_of(z, b + 4 * h, 0) for z in range(NZ) for h in range(2)] for b in range(4)
] + [[row_of(j + 4 * i, y, 1) for i in range(3) for y in range(NY)] for j in range(4)]
GROUP = 24
PLANE_GROUPS = [[row_of(z, j // 2, j % 2) for j in range(NY * NC)] for z in range(NZ)]
Z_GROUPS = [[row_of(z, j // 2, j % 2) for z in range(NZ)] for j in range(NY * NC)]
UP = [(x, (x + 1) % NX) for x in range(NX)]
DOWN = [((x + 1) % NX, x) for x in range(NX)]
CORE_GROUPS = [[r, r + 1] for r in range(0, NZ * NY * NC, NC)]


def pack_kernel(fill_ref, panel_ref, slab_hbm, out_ref, copies_ref, slab_ref, sems):
    sections, rows = slab_ref.shape[0], slab_ref.shape[1] // TILE
    fetches = []
    for group in range(sections * rows):
        block = (group // rows, pl.ds(group % rows * TILE, TILE))
        fetches.append(
            pltpu.make_async_copy(slab_hbm.at[block], slab_ref.at[block], sems.at[group])
        )
        fetches[-1].start()
    for copy in range(copies_ref.shape[0]):
        copies_ref[copy] = panel_ref[...]
    cols = slab_ref.shape[2] // TILE
    lane = lax.broadcasted_iota(jnp.int32, (TAIL, TILE), 1)
    words = jnp.zeros((TAIL, TILE), jnp.float32)
    for group in range(sections * rows):
        s, r = group // rows, group % rows
        count = jnp.int32(0)
        for k in range(cols):
            count += fill_ref[s, r, k]
        fetches[group].wait()
        seen = jnp.int32(0)
        for k in range(cols):
            filled = fill_ref[s, r, k]
            slot = jnp.where(filled == 1, seen, count + k - seen)
            seen += filled

            @pl.when(slot < SLOTS)
            def _(group=group, s=s, r=r, k=k, slot=slot):
                column = pl.multiple_of(slot * TILE, TILE)
                out_ref[pl.ds(group * TILE, TILE), pl.ds(column, TILE)] = slab_ref[
                    s, r * TILE : (r + 1) * TILE, k * TILE : (k + 1) * TILE
                ]

            place = jnp.where(slot < SLOTS, group * (SLOTS + 1) + slot, -1)
            words = jnp.where(lane == place, jnp.float32(k), words)
        words = jnp.where(lane == group * (SLOTS + 1) + SLOTS, count.astype(jnp.float32), words)
    tail = slice(sections * rows * TILE, sections * rows * TILE + TAIL)
    out_ref[tail, :] = jnp.zeros((TAIL, SLOTS * TILE), jnp.bfloat16)
    out_ref[tail, :TILE] = words.astype(jnp.bfloat16)


def pack(slab, slab_fill, panel):
    sections, rows, cols = slab.shape
    height = sections * rows + TAIL
    vmem = pl.BlockSpec(memory_space=pltpu.VMEM)
    return pl.pallas_call(
        pack_kernel,
        out_shape=(
            jax.ShapeDtypeStruct((height, SLOTS * TILE), jnp.bfloat16),
            jax.ShapeDtypeStruct((GROUP,) + panel.shape, jnp.bfloat16),
        ),
        in_specs=[pl.BlockSpec(memory_space=pltpu.SMEM), vmem, pl.BlockSpec(memory_space=pl.ANY)],
        out_specs=(vmem, vmem),
        scratch_shapes=[
            pltpu.VMEM((sections, rows, cols), jnp.bfloat16),
            pltpu.SemaphoreType.DMA((sections * rows // TILE,)),
        ],
        cost_estimate=pl.CostEstimate(flops=0, bytes_accessed=2 * 2**20, transcendentals=0),
    )(slab_fill, panel, slab)


def product_kernel(place_ref, words_ref, keep_ref, *refs):
    lefts, pieces = refs[:NX], refs[NX : NX + 4]
    out_ref, sums_ref, right_ref, near_ref = refs[NX + 4 :]
    sections = right_ref.shape[0]
    row, col = place_ref[0], place_ref[1]
    z, y = row // (NY * NC), (row // NC) % NY
    for step, piece in enumerate(pieces):
        if SHIFTS[step] == 2:
            y_from = jnp.where(y % 2 == 0, y - 2, y + 2)
            z_from = jnp.where(z % 2 == 0, z - 2, z + 2)
        else:
            y_from, z_from = y - SHIFTS[step], z - SHIFTS[step]
        first_y, first_z = (y_from + NY) % 4 * 64, (z_from + NZ) % 4 * 512
        for slot in range(GROUP):
            at_y = first_y + (slot // 2 * 512 + slot % 2 * 256)
            at_z = first_z + (slot // 8 * 2048 + slot % 8 * 64 + DEPTH)
            for core, at in enumerate((at_y, at_z)):
                rows = pl.ds(pl.multiple_of(at, DEPTH), DEPTH)
                for s in range(sections):
                    right_ref[s, rows] = piece[core, slot, s]

    row_blocks = out_ref.shape[0] // TILE
    per_source = sections * row_blocks * (SLOTS + 1)
    colsum = jnp.zeros((8, TILE), jnp.float32)
    for r in range(row_blocks):
        total = jnp.zeros((TILE, TILE), jnp.float32)
        for source in range(NX):
            block_col = (col + (0, NX - 1, 1, 2)[source]) % NX
            for s in range(sections):
                group = s * row_blocks + r
                base = source * per_source + group * (SLOTS + 1)
                count = words_ref[base + SLOTS]
                for slot in range(SLOTS):
                    tile = block_col * 12 + words_ref[base + slot]
                    rows = pl.ds(pl.multiple_of(tile * TILE, TILE), TILE)
                    keep = (slot < count).astype(jnp.float32).astype(jnp.bfloat16)
                    near_ref[slot * TILE : (slot + 1) * TILE] = right_ref[s, rows] * keep
                left = lefts[source][group * TILE : (group + 1) * TILE, :]
                total += jnp.dot(left, near_ref[...], preferred_element_type=jnp.float32)
        squares = total * total * keep_ref[r].astype(jnp.float32)
        out_ref[r * TILE : (r + 1) * TILE] = squares
        colsum += jnp.sum(squares.reshape(TILE // 8, 8, TILE), axis=0)
    sums_ref[...] = jnp.broadcast_to(colsum[None], sums_ref.shape)


def multiply(place, words, keep, lefts, pieces, sections, rows):
    smem = pl.BlockSpec(memory_space=pltpu.SMEM)
    vmem = pl.BlockSpec(memory_space=pltpu.VMEM)
    depth = NZ * NY * NC * DEPTH
    return pl.pallas_call(
        product_kernel,
        out_shape=(
            jax.ShapeDtypeStruct((rows, TILE), jnp.float32),
            jax.ShapeDtypeStruct((NY * NC, 8, TILE), jnp.float32),
        ),
        in_specs=[smem, smem, smem] + [vmem] * (NX + 4),
        out_specs=(vmem, vmem),
        scratch_shapes=[
            pltpu.VMEM((sections, depth, TILE), jnp.bfloat16),
            pltpu.VMEM((SLOTS * TILE, TILE), jnp.bfloat16),
        ],
        compiler_params=pltpu.CompilerParams(vmem_limit_bytes=32 * 2**20),
        cost_estimate=pl.CostEstimate(
            flops=sections * rows * depth * TILE, bytes_accessed=7 * 2**20, transcendentals=0
        ),
    )(place, words, keep, *lefts, *pieces)


def shards(slab, slab_fill, panel, out_fill):
    sections, row_count, local_cols = slab.shape
    place = jnp.stack([lax.axis_index("row"), lax.axis_index("col")]).astype(jnp.int32)
    packed, copies = pack(slab, slab_fill, panel)
    held = lax.all_to_all(copies, "row", 0, 0, tiled=True, axis_index_groups=MIXED_GROUPS)
    below = lax.ppermute(packed, "col", UP)
    above = lax.ppermute(packed, "col", DOWN)
    across = lax.ppermute(below, "col", UP)
    mine = [held] + [lax.ppermute(held, "row", shift_moves(s)) for s in SHIFTS[1:]]
    moved, (above, across) = lax.optimization_barrier((mine[1:], (above, across)))
    mine = [held] + moved
    lefts = [packed, below, above, across]
    pieces = [lax.all_gather(piece, "row", axis_index_groups=CORE_GROUPS) for piece in mine]
    tail = sections * row_count
    count = sections * row_count // TILE * (SLOTS + 1)
    words = jnp.concatenate([left[tail, :count] for left in lefts]).astype(jnp.int32)
    squares, sums = multiply(
        place, words, out_fill.reshape(-1), lefts, pieces, sections, row_count
    )
    sums = lax.all_to_all(sums, "row", 0, 0, tiled=True, axis_index_groups=PLANE_GROUPS)
    sums = jnp.sum(sums, axis=0)
    sums = jnp.sum(spread(sums, "row", NZ, Z_GROUPS), axis=(0, 1))
    factor_col = jnp.float32(row_count * NZ * NY * NC) / sums
    return squares * factor_col


def solution(mesh):
    placed = (P(None, "row", "col"), P(None, "row", "col"), P(None, "row", "col"), P("row", "col"))
    return jax.shard_map(
        shards, mesh=mesh, in_specs=placed, out_specs=P("row", "col"), check_vma=False
    )
```

```python
import jax
import jax.numpy as jnp
from jax import lax
from jax.experimental import pallas as pl
from jax.experimental.pallas import tpu as pltpu
from jax.sharding import PartitionSpec as P

TILE = 128
NZ, NY, NC, NX = 12, 8, 2, 4
DEPTH = 32
SLOTS = 6
TAIL = 16
HALF = 2


def row_of(z, y, core):
    return (z % NZ) * NY * NC + (y % NY) * NC + core


def spread(piece, axis, size, groups):
    copies = jnp.broadcast_to(piece[None], (size,) + piece.shape)
    return lax.all_to_all(copies, axis, 0, 0, tiled=True, axis_index_groups=groups)


def step_of(position, shift):
    if shift == 2:
        return 2 if position % 2 == 0 else -2
    return shift


def shift_moves(shift):
    moves = []
    for z in range(NZ):
        for y in range(NY):
            moves.append((row_of(z, y, 0), row_of(z, y + step_of(y, shift), 0)))
            moves.append((row_of(z, y, 1), row_of(z + step_of(z, shift), y, 1)))
    return moves


SHIFTS = (0, 2, 1, -1)
MIXED_GROUPS = [
    [row_of(z, b + 4 * h, 0) for z in range(NZ) for h in range(2)] for b in range(4)
] + [[row_of(j + 4 * i, y, 1) for i in range(3) for y in range(NY)] for j in range(4)]
GROUP = 24
PLANE_GROUPS = [[row_of(z, j // 2, j % 2) for j in range(NY * NC)] for z in range(NZ)]
Z_GROUPS = [[row_of(z, j // 2, j % 2) for z in range(NZ)] for j in range(NY * NC)]
UP = [(x, (x + 1) % NX) for x in range(NX)]
DOWN = [((x + 1) % NX, x) for x in range(NX)]
CORE_GROUPS = [[r, r + 1] for r in range(0, NZ * NY * NC, NC)]


def pack_kernel(fill_ref, panel_ref, slab_hbm, out_ref, copies_ref, slab_ref, sems):
    sections, rows = slab_ref.shape[0], slab_ref.shape[1] // TILE
    fetches = []
    for group in range(sections * rows):
        block = (group // rows, pl.ds(group % rows * TILE, TILE))
        fetches.append(
            pltpu.make_async_copy(slab_hbm.at[block], slab_ref.at[block], sems.at[group])
        )
        fetches[-1].start()
    for copy in range(copies_ref.shape[0]):
        copies_ref[copy] = panel_ref[...]
    cols = slab_ref.shape[2] // TILE
    lane = lax.broadcasted_iota(jnp.int32, (TAIL, TILE), 1)
    words = jnp.zeros((TAIL, TILE), jnp.float32)
    for group in range(sections * rows):
        s, r = group // rows, group % rows
        count = jnp.int32(0)
        for k in range(cols):
            count += fill_ref[s, r, k]
        fetches[group].wait()
        seen = jnp.int32(0)
        for k in range(cols):
            filled = fill_ref[s, r, k]
            slot = jnp.where(filled == 1, seen, count + k - seen)
            seen += filled

            @pl.when(slot < SLOTS)
            def _(group=group, s=s, r=r, k=k, slot=slot):
                column = pl.multiple_of(slot * TILE, TILE)
                out_ref[pl.ds(group * TILE, TILE), pl.ds(column, TILE)] = slab_ref[
                    s, r * TILE : (r + 1) * TILE, k * TILE : (k + 1) * TILE
                ]

            place = jnp.where(slot < SLOTS, group * (SLOTS + 1) + slot, -1)
            words = jnp.where(lane == place, jnp.float32(k), words)
        words = jnp.where(lane == group * (SLOTS + 1) + SLOTS, count.astype(jnp.float32), words)
    tail = slice(sections * rows * TILE, sections * rows * TILE + TAIL)
    out_ref[tail, :] = jnp.zeros((TAIL, SLOTS * TILE), jnp.bfloat16)
    out_ref[tail, :TILE] = words.astype(jnp.bfloat16)


def pack(slab, slab_fill, panel):
    sections, rows, cols = slab.shape
    height = sections * rows + TAIL
    vmem = pl.BlockSpec(memory_space=pltpu.VMEM)
    return pl.pallas_call(
        pack_kernel,
        out_shape=(
            jax.ShapeDtypeStruct((height, SLOTS * TILE), jnp.bfloat16),
            jax.ShapeDtypeStruct((GROUP,) + panel.shape, jnp.bfloat16),
        ),
        in_specs=[pl.BlockSpec(memory_space=pltpu.SMEM), vmem, pl.BlockSpec(memory_space=pl.ANY)],
        out_specs=(vmem, vmem),
        scratch_shapes=[
            pltpu.VMEM((sections, rows, cols), jnp.bfloat16),
            pltpu.SemaphoreType.DMA((sections * rows // TILE,)),
        ],
        cost_estimate=pl.CostEstimate(flops=0, bytes_accessed=2 * 2**20, transcendentals=0),
    )(slab_fill, panel, slab)


def product_kernel(place_ref, words_ref, keep_ref, *refs):
    lefts, pieces = refs[:NX], refs[NX : NX + 4]
    out_ref, sums_ref, right_ref, near_ref = refs[NX + 4 :]
    sections = right_ref.shape[0]
    row, col = place_ref[0], place_ref[1]
    z, y = row // (NY * NC), (row // NC) % NY
    for step, piece in enumerate(pieces):
        if SHIFTS[step] == 2:
            y_from = jnp.where(y % 2 == 0, y - 2, y + 2)
            z_from = jnp.where(z % 2 == 0, z - 2, z + 2)
        else:
            y_from, z_from = y - SHIFTS[step], z - SHIFTS[step]
        first_y, first_z = (y_from + NY) % 4 * 64, (z_from + NZ) % 4 * 512
        for slot in range(GROUP):
            at_y = first_y + (slot // 2 * 512 + slot % 2 * 256)
            at_z = first_z + (slot // 8 * 2048 + slot % 8 * 64 + DEPTH)
            for core, at in enumerate((at_y, at_z)):
                rows = pl.ds(pl.multiple_of(at, DEPTH), DEPTH)
                for s in range(sections):
                    right_ref[s, rows] = piece[core, slot, s]

    row_blocks = out_ref.shape[0] // TILE
    per_source = sections * row_blocks * (SLOTS + 1)
    colsum = jnp.zeros((8, TILE), jnp.float32)
    for r in range(row_blocks):
        total = jnp.zeros((TILE, TILE), jnp.float32)
        for source in range(NX):
            block_col = (col + (0, NX - 1, 1, 2)[source]) % NX
            for s in range(sections):
                group = s * row_blocks + r
                base = source * per_source + group * (SLOTS + 1)
                count = words_ref[base + SLOTS]
                for slot in range(SLOTS):
                    tile = block_col * 12 + words_ref[base + slot]
                    rows = pl.ds(pl.multiple_of(tile * TILE, TILE), TILE)
                    keep = (slot < count).astype(jnp.float32).astype(jnp.bfloat16)
                    near_ref[s % 2, slot * TILE : (slot + 1) * TILE] = right_ref[s, rows] * keep
                left = lefts[source][group * TILE : (group + 1) * TILE, :]
                total += jnp.dot(left, near_ref[s % 2], preferred_element_type=jnp.float32)
        squares = total * total * keep_ref[r].astype(jnp.float32)
        out_ref[r * TILE : (r + 1) * TILE] = squares
        colsum += jnp.sum(squares.reshape(TILE // 8, 8, TILE), axis=0)
    sums_ref[...] = jnp.broadcast_to(colsum[None], sums_ref.shape)


def multiply(place, words, keep, lefts, pieces, sections, rows):
    smem = pl.BlockSpec(memory_space=pltpu.SMEM)
    vmem = pl.BlockSpec(memory_space=pltpu.VMEM)
    depth = NZ * NY * NC * DEPTH
    return pl.pallas_call(
        product_kernel,
        out_shape=(
            jax.ShapeDtypeStruct((rows, TILE), jnp.float32),
            jax.ShapeDtypeStruct((NY * NC, 8, TILE), jnp.float32),
        ),
        in_specs=[smem, smem, smem] + [vmem] * (NX + 4),
        out_specs=(vmem, vmem),
        scratch_shapes=[
            pltpu.VMEM((sections, depth, TILE), jnp.bfloat16),
            pltpu.VMEM((2, SLOTS * TILE, TILE), jnp.bfloat16),
        ],
        compiler_params=pltpu.CompilerParams(vmem_limit_bytes=32 * 2**20),
        cost_estimate=pl.CostEstimate(
            flops=sections * rows * depth * TILE, bytes_accessed=7 * 2**20, transcendentals=0
        ),
    )(place, words, keep, *lefts, *pieces)


def shards(slab, slab_fill, panel, out_fill):
    sections, row_count, local_cols = slab.shape
    place = jnp.stack([lax.axis_index("row"), lax.axis_index("col")]).astype(jnp.int32)
    packed, copies = pack(slab, slab_fill, panel)
    held = lax.all_to_all(copies, "row", 0, 0, tiled=True, axis_index_groups=MIXED_GROUPS)
    below = lax.ppermute(packed, "col", UP)
    above = lax.ppermute(packed, "col", DOWN)
    across = lax.ppermute(below, "col", UP)
    mine = [held] + [lax.ppermute(held, "row", shift_moves(s)) for s in SHIFTS[1:]]
    moved, (above, across) = lax.optimization_barrier((mine[1:], (above, across)))
    mine = [held] + moved
    lefts = [packed, below, above, across]
    pieces = [lax.all_gather(piece, "row", axis_index_groups=CORE_GROUPS) for piece in mine]
    tail = sections * row_count
    count = sections * row_count // TILE * (SLOTS + 1)
    words = jnp.concatenate([left[tail, :count] for left in lefts]).astype(jnp.int32)
    squares, sums = multiply(
        place, words, out_fill.reshape(-1), lefts, pieces, sections, row_count
    )
    sums = lax.all_to_all(sums, "row", 0, 0, tiled=True, axis_index_groups=PLANE_GROUPS)
    sums = jnp.sum(sums, axis=0)
    sums = jnp.sum(spread(sums, "row", NZ, Z_GROUPS), axis=(0, 1))
    factor_col = jnp.float32(row_count * NZ * NY * NC) / sums
    return squares * factor_col


def solution(mesh):
    placed = (P(None, "row", "col"), P(None, "row", "col"), P(None, "row", "col"), P("row", "col"))
    return jax.shard_map(
        shards, mesh=mesh, in_specs=placed, out_specs=P("row", "col"), check_vma=False
    )
```
